128 devices in a mesh: group: 8 (over y, core), expert: 16 (over z, x).
Axes of the slice: x: 4, y: 4, z: 4, core: 2. Of those that a mesh axis runs over, the one named last changes fastest.
Arguments:
- tokens: bfloat16 [4096, 2048], P(('group', 'expert')), may hold values from -6 to 6
- out_grad: bfloat16 [4096, 2048], P(('group', 'expert')), may hold values from -6 to 6
- expert_ids: int32 [4096, 8], P(('group', 'expert')), may hold values from 0 to 255, as said below
- gate_w: bfloat16 [4096, 8], P(('group', 'expert')), may hold values from 0.049804688 to 0.59765625
- query_ids: int32 [128, 32], P(('group', 'expert')), may hold values from 0 to 7, never falling along the last dimension, each value on 1 to 8 neighbouring positions
- w_gate: bfloat16 [256, 2048, 512], P(('group', 'expert')), may hold values from -0.125 to 0.125
- w_up: bfloat16 [256, 2048, 512], P(('group', 'expert')), may hold values from -0.125 to 0.125
- w_down: bfloat16 [256, 512, 2048], P(('group', 'expert')), may hold values from -0.25 to 0.25
- proj_out: bfloat16 [256, 2048, 64], P(('group', 'expert')), may hold values from -0.125 to 0.125
- proj_in: bfloat16 [256, 512, 64], P(('group', 'expert')), may hold values from -0.25 to 0.25
- train_grads: bfloat16 [256, 4096, 512], P(('group', 'expert')), may hold values from -0.09375 to 0.09375
Outputs:
- token_grads: bfloat16 [4096, 2048], P(('group', 'expert'))
- scores: float32 [1024, 512], P(('group', 'expert'))
The draws below stay inside these ranges and needn't reach their ends.
Inputs may be any that keep to these rules, and one draw needn't show every extreme that they name: `expert_ids`: each token names 8 different experts, two in each of 4 different groups, a group being 32 consecutive experts. Among the 32 tokens of one block every group is named by exactly 16 tokens and every expert by at most 2 tokens; in every block some expert is named by exactly 2. `query_ids`: along one block's tokens the query number never falls; each of the 8 queries of a block has 1 to 8 tokens, and one has exactly 8.
All inputs are finite; a program needn't handle non-finite values.
Results may differ from the reference program's by a relative error of at most 0.0064.
Values may be sent and summed in bfloat16 or wider, within the bound.
A program may use at most 128 MiB of HBM per device.

```python
import math
import jax
import jax.numpy as jnp
import numpy as np
from jax import lax

D = 2048
F = 512
RANK = 64
TRAIN = 512
TOK_DEV = 32
QRY_DEV = 8
GROUPS = 8
EXP_GROUP = 32
EXPERTS = 256
GROUP_TOP = 4
TOP = 8
CAP = 2
BLOCKS = 128
TOKENS = 4096
QUERIES = 1024
QMOST = 8


def draw_expert_ids(key, part):
    blocks = TOKENS // TOK_DEV
    hot_count = EXP_GROUP // 4
    key_list = jax.random.split(key, 5)
    position = jax.vmap(lambda key_one: jax.random.permutation(key_one, TOK_DEV))(jax.random.split(key_list[0], blocks))
    group_perm = jax.vmap(lambda key_one: jax.random.permutation(key_one, GROUPS))(jax.random.split(key_list[1], blocks))
    local_perm = jax.vmap(lambda key_one: jax.random.permutation(key_one, EXP_GROUP))(jax.random.split(key_list[2], GROUPS))
    spread = jax.random.randint(key_list[3], (blocks, 1), 2 * hot_count, EXP_GROUP - hot_count + 1)
    offset = jax.random.randint(key_list[4], (blocks, 1), 0, EXP_GROUP)
    parity = position % 2
    half_pos = position // 2
    choose = (parity[:, :, None] + 2 * jnp.arange(GROUP_TOP)[None, None, :]) % GROUPS
    group_ids = jnp.take_along_axis(jnp.broadcast_to(group_perm[:, None, :], (blocks, TOK_DEV, GROUPS)), choose, axis=2)
    first_local = half_pos % hot_count
    second_local = hot_count + (half_pos + offset) % spread
    first_expert = local_perm[group_ids, first_local[:, :, None]]
    second_expert = local_perm[group_ids, second_local[:, :, None]]
    experts = group_ids[:, :, :, None] * EXP_GROUP + jnp.stack([first_expert, second_expert], axis=3)
    return experts.reshape(TOKENS, TOP).astype(jnp.int32)


def level_of(key, extent, shards, smallest, high):
    loudness = 1.0
    for dim, parts in shards:
        draws = jax.random.uniform(jax.random.fold_in(jax.random.fold_in(key, 6), dim), (parts,), jnp.float32, smallest / len(shards), high / len(shards))
        loudness = loudness * jnp.repeat(jnp.exp(draws), extent[dim] // parts).reshape((-1,) + (1,) * (len(extent) - 1 - dim))
    return loudness


def length_profile(count, total, most, slope):
    weights = [(1 << 20) // math.isqrt(standing ** slope) + 1 for standing in range(2, count + 1)]
    surplus, holding = total - most - (count - 1), [1] * (count - 1)
    while surplus > 0:
        free = [i for i in range(count - 1) if holding[i] < most]
        mass, budget = sum([weights[i] for i in free]), surplus
        for i in free:
            more = min(most - holding[i], max(1, budget * weights[i] // mass), surplus)
            holding[i] = holding[i] + more
            surplus = surplus - more
    return np.array([most] + holding)


def ragged_sizes(rng, count, total, bound, lean):
    if count == 2:
        one = jax.random.randint(rng, (), max(1, total - bound), min(bound, total - 1) + 1)
        return jnp.stack([one, total - one])
    sizes = jnp.asarray(length_profile(count, total, bound, lean), jnp.int32)
    couples = (count - 1) // 2
    source_of, taker = sizes[1:1 + 2 * couples:2], sizes[2:2 + 2 * couples:2]
    room = jnp.minimum(source_of - 1, bound - taker)
    shifted = jax.random.randint(jax.random.fold_in(rng, 1), (couples,), 0, 1 << 20) % (room + 1)
    sizes = sizes.at[1:1 + 2 * couples:2].set(source_of - shifted).at[2:2 + 2 * couples:2].set(taker + shifted)
    return sizes[jax.random.permutation(jax.random.fold_in(rng, 2), count)]


def centred(own_key, dims, scale, limit, cuts=(), kind=jnp.bfloat16):
    factor_of = level_of(own_key, dims, cuts, -0.22, 0.18) if cuts else 1.0
    entries = jax.random.normal(own_key, dims, jnp.float32) * scale * factor_of
    return jnp.minimum(jnp.maximum(entries, -limit), limit).astype(kind)


def setup_inputs(seed: int = 0) -> dict:
    key_of = jax.random.split(jax.random.key(seed), 12)
    tokens = centred(key_of[0], (TOKENS, D), 1.0, 6.0, ((0, 128),))
    out_grad = centred(key_of[1], (TOKENS, D), 1.0, 6.0, ((0, 128),))
    expert_ids = draw_expert_ids(jax.random.fold_in(key_of[11], 71), 0)
    gate_w = jnp.clip(0.049804688 + 0.54785156 * jax.random.uniform(key_of[3], (TOKENS, TOP), jnp.float32) ** level_of(key_of[3], (TOKENS, TOP), ((0, 128),), -0.2, 0.2), 0.049804688, 0.59765625).astype(jnp.bfloat16)
    query_ids = jax.vmap(lambda own: jnp.searchsorted(jnp.cumsum(ragged_sizes(own, QRY_DEV, TOK_DEV, QMOST, 2)), jnp.arange(TOK_DEV), side="right"))(jax.random.split(key_of[4], BLOCKS)).reshape((BLOCKS, TOK_DEV)).astype(jnp.int32)
    w_gate = centred(key_of[5], (EXPERTS, D, F), D ** -0.5, 0.125, ((0, 128),))
    w_up = centred(key_of[6], (EXPERTS, D, F), D ** -0.5, 0.125, ((0, 128),))
    w_down = centred(key_of[7], (EXPERTS, F, D), F ** -0.5, 0.25, ((0, 128),))
    proj_out = centred(key_of[8], (EXPERTS, D, RANK), D ** -0.5, 0.125, ((0, 128),))
    proj_in = centred(key_of[9], (EXPERTS, F, RANK), F ** -0.5, 0.25, ((0, 128),))
    train_grads = centred(key_of[10], (EXPERTS, RANK * RANK, TRAIN), (RANK * RANK) ** -0.5, 0.09375, ((0, 128),))
    return {"tokens": tokens, "out_grad": out_grad, "expert_ids": expert_ids, "gate_w": gate_w, "query_ids": query_ids, "w_gate": w_gate, "w_up": w_up, "w_down": w_down, "proj_out": proj_out, "proj_in": proj_in, "train_grads": train_grads}


def pair_terms(rows_x, rows_g, rows_w, gate_mat, up_mat, down_mat, left_proj, right_proj, stored):
    contract = (((1,), (1,)), ((), ()))
    a_gate = jnp.dot(rows_x, gate_mat, preferred_element_type=jnp.float32)
    a_up = jnp.dot(rows_x, up_mat, preferred_element_type=jnp.float32)
    sigmoid_val = jax.nn.sigmoid(a_gate)
    active = a_gate * sigmoid_val
    hidden = (active * a_up).astype(jnp.bfloat16)
    delta_rows = (rows_w.astype(jnp.float32)[:, None] * rows_g.astype(jnp.float32)).astype(jnp.bfloat16)
    d_hidden = lax.dot_general(delta_rows, down_mat, contract, preferred_element_type=jnp.float32)
    grad_up = (d_hidden * active).astype(jnp.bfloat16)
    grad_gate = (d_hidden * a_up * sigmoid_val * (1.0 + a_gate * (1.0 - sigmoid_val))).astype(jnp.bfloat16)
    pair_grad = lax.dot_general(grad_gate, gate_mat, contract, preferred_element_type=jnp.float32)
    pair_grad = pair_grad + lax.dot_general(grad_up, up_mat, contract, preferred_element_type=jnp.float32)
    left_vec = jnp.dot(delta_rows, left_proj, preferred_element_type=jnp.float32)
    right_vec = jnp.dot(hidden, right_proj, preferred_element_type=jnp.float32)
    outer_prod = (left_vec[:, :, None] * right_vec[:, None, :]).reshape(left_vec.shape[0], -1).astype(jnp.bfloat16)
    pair_score = jnp.dot(outer_prod, stored, preferred_element_type=jnp.float32)
    return pair_grad.astype(jnp.bfloat16), pair_score


def reference(tokens, out_grad, expert_ids, gate_w, query_ids, w_gate, w_up, w_down, proj_out, proj_in, train_grads):
    pair_total = TOKENS * TOP
    flat_experts = expert_ids.reshape(-1).astype(jnp.int32)
    sorting = jnp.argsort(flat_experts, stable=True).astype(jnp.int32)
    counts = jnp.zeros((EXPERTS,), jnp.int32).at[flat_experts].add(1)
    starts = (jnp.cumsum(counts) - counts).astype(jnp.int32)
    room = BLOCKS * CAP
    flat_weights = gate_w.reshape(-1)

    def expert_step(carried, expert):
        grad_sum, score_sum = carried
        offsets = jnp.arange(room, dtype=jnp.int32)
        used = offsets < counts[expert]
        pair_index = sorting[jnp.minimum(starts[expert] + offsets, pair_total - 1)]
        token_index = (pair_index // TOP).astype(jnp.int32)
        rows_w = jnp.where(used, flat_weights[pair_index], jnp.zeros((), flat_weights.dtype))
        pair_grad, pair_score = pair_terms(tokens[token_index], out_grad[token_index], rows_w, w_gate[expert], w_up[expert], w_down[expert], proj_out[expert], proj_in[expert], train_grads[expert])
        grad_sum = grad_sum.at[token_index].add(pair_grad.astype(jnp.float32))
        score_sum = score_sum.at[token_index].add(pair_score)
        return (grad_sum, score_sum), None

    initial = (jnp.zeros((TOKENS, D), jnp.float32), jnp.zeros((TOKENS, TRAIN), jnp.float32))
    (grad_sum, score_sum), _ = lax.scan(expert_step, initial, jnp.arange(EXPERTS, dtype=jnp.int32))
    block_of = (jnp.arange(TOKENS, dtype=jnp.int32) // TOK_DEV).astype(jnp.int32)
    query_global = (block_of * QRY_DEV + query_ids.reshape(-1)).astype(jnp.int32)
    scores = jax.ops.segment_sum(score_sum, query_global, num_segments=QUERIES)
    return grad_sum.astype(jnp.bfloat16), scores
```

```python
import jax
import jax.numpy as jnp
from jax import lax
from jax.experimental import pallas as pl
from jax.experimental.pallas import tpu as pltpu
from jax.sharding import PartitionSpec as P

MESH = pl.DeviceIdType.MESH
BF = jnp.bfloat16
F32 = jnp.float32
COLS = ((0, 640), (640, 1280), (1280, 2048))
SCOLS = ((0, 256), (256, 512), None)
WIDTH = tuple(b - a for a, b in COLS)
D = 2048
F = 512
TRAIN = 512


def nn(a, b):
    return jnp.dot(a, b, preferred_element_type=F32)


def nt(a, b):
    return lax.dot_general(a, b, (((1,), (1,)), ((), ())), preferred_element_type=F32)


def tn(a, b):
    return lax.dot_general(a, b, (((0,), (0,)), ((), ())), preferred_element_type=F32)


def coords(axis, line, u, v):
    return ((line, u, v), (u, line, v), (u, v, line))[axis]


def device(axis, line, u, v, core):
    y, z, x = coords(axis, line, u, v)
    return (y * 2 + core, z * 4 + x)


def expert_of(axis, line, u, v, core, which):
    group, place = device(axis, line, u, v, core)
    return group * 32 + place * 2 + which


def aligned(start, unit):
    return pl.ds(pl.multiple_of(start * unit, unit), unit)


def kernel(
    tok, og, ids_ref, gw_ref, qid_ref, wg_h, wu_h, wd_h, po_h, pi_h, tr_h,
    grads_out, scores_out,
    wg, wu, wd, po, pi, tr,
    meta, perm, pick, pickw,
    tx0, tx1, tx2, tg0, tg1, tg2,
    sx0, sx1, sx2, sd0, sd1, sd2,
    rx0, rx1, rx2, rd0, rd1, rd2,
    xc, hid, fa, fb, right, gg, gu, gc, outer, scc,
    gs0, gs1, gs2, gr0, gr1, gr2,
    ss0, ss1, sr0, sr1,
    pg0, pg1, pg2, hg0, hg1, hg2, pq0, pq1, hq0, hq1,
    load_sem, send_sem, recv_sem,
):
    tx, tg = (tx0, tx1, tx2), (tg0, tg1, tg2)
    sx, sd = (sx0, sx1, sx2), (sd0, sd1, sd2)
    rx, rd = (rx0, rx1, rx2), (rd0, rd1, rd2)
    gs, gr = (gs0, gs1, gs2), (gr0, gr1, gr2)
    ss, sr = (ss0, ss1), (sr0, sr1)
    pg, hg = (pg0, pg1, pg2), (hg0, hg1, hg2)
    pq, hq = (pq0, pq1), (hq0, hq1)
    group, place = lax.axis_index("group"), lax.axis_index("expert")
    y, core = group // 2, group % 2
    z, x = place // 4, place % 4
    line = (y, z, x)
    uv = ((z, x), (y, x), (y, z))
    plane = tuple((u * 4 + v) * 2 + core for u, v in uv)

    loads = [
        pltpu.make_async_copy(src, dst, load_sem.at[n])
        for n, (src, dst) in enumerate(
            (
                (wg_h, wg), (wu_h, wu), (pi_h, pi.at[:, 0:64]), (pi_h, pi.at[:, 64:128]),
                (wd_h, wd), (po_h, po), (tr_h, tr),
            )
        )
    ]

    barrier = pltpu.get_barrier_semaphore()
    for a in range(3):
        def greet(j, carry, a=a):
            t = (plane[a] + j) % 32
            pl.semaphore_signal(
                barrier, inc=1, device_id=device(a, line[a], t // 8, (t // 2) % 4, t % 2), device_id_type=MESH
            )
            return carry
        lax.fori_loop(1, 32, greet, 0)
    for load in loads:
        load.start()

    own = jnp.concatenate([ids_ref[...].astype(F32), gw_ref[...].astype(F32)], axis=0).astype(BF)
    for a in range(3):
        lane = lax.broadcasted_iota(jnp.int32, (32, 128), 1)
        row = lax.broadcasted_iota(jnp.int32, (32, 128), 0)
        put = jnp.where(lane == row + 32 * line[a], 1.0, 0.0).astype(BF)
        meta[a, pl.ds(line[a], 1)] = nn(own, put).astype(BF)[None]
    pl.semaphore_wait(barrier, 93)

    def line_peers(a):
        for d in range(1, 4):
            there = (line[a] + d) % 4
            yield there, device(a, there, uv[a][0], uv[a][1], core)

    def on_line(a, src_of, dst, phase):
        sem = phase * 3 + a
        for there, dev in line_peers(a):
            pltpu.make_async_remote_copy(
                src_of(there), dst, send_sem.at[sem], recv_sem.at[sem], device_id=dev, device_id_type=MESH
            ).start()

    def wait_bytes(ref, sem):
        pltpu.make_async_copy(ref, ref, sem).wait()

    for a in range(3):
        on_line(a, lambda there, a=a: meta.at[a, line[a]], meta.at[a, line[a]], 0)
    for phase, src, dst in ((1, tok, tx), (2, og, tg)):
        for a in range(3):
            part = src.at[:, COLS[a][0]:COLS[a][1]]
            spot = dst[a].at[aligned(line[a], 32)]
            on_line(a, lambda there, part=part: part, spot, phase)
            pltpu.make_async_copy(part, spot, recv_sem.at[phase * 3 + a]).start()

    for a in range(3):
        def order(q, carry, a=a):
            n = lax.broadcasted_iota(jnp.int32, (64, 512), 0) + q * 64
            lane = lax.broadcasted_iota(jnp.int32, (64, 512), 1)
            which, low, c0 = n // 256, n % 2, (n // 2) % 2
            ny, nz, nx = (n // 64) % 4, (n // 16) % 4, (n // 4) % 4
            l0, u0, v0 = ((ny, nz, nx), (nz, ny, nx), (nx, ny, nz))[a]
            at = ((u0 * 4 + v0) * 2 + c0) * 16 + which * 8 + l0 * 2 + low
            perm[a, aligned(q, 64)] = jnp.where(lane == at, 1.0, 0.0).astype(BF)
            return carry
        lax.fori_loop(0, 8, order, 0)

    for a in range(3):
        wait_bytes(meta.at[a, 0:3], recv_sem.at[a])
        both = (meta[a, 0].astype(F32) + meta[a, 1].astype(F32)) + (meta[a, 2].astype(F32) + meta[a, 3].astype(F32))
        r0 = lax.broadcasted_iota(jnp.int32, (128, 128), 0)
        c1 = lax.broadcasted_iota(jnp.int32, (128, 128), 1)
        before = jnp.where((r0 < c1) & (r0 // 32 == c1 // 32), 1.0, 0.0).astype(BF)

        def slots(q, carry, a=a, both=both, before=before):
            n = lax.broadcasted_iota(jnp.int32, (128, 128), 0) + q * 128
            lane = lax.broadcasted_iota(jnp.int32, (128, 128), 1)
            u0, v0, c0, which = n // 128, (n // 32) % 4, (n // 16) % 2, (n // 8) % 2
            wanted = expert_of(a, line[a], u0, v0, c0, which).astype(F32)
            named = jnp.zeros((128, 128), F32)
            weight = jnp.zeros((128, 128), F32)
            for k in range(8):
                hit = both[k:k + 1, :] == wanted
                named = named + jnp.where(hit, 1.0, 0.0)
                weight = weight + jnp.where(hit, both[8 + k:9 + k, :], 0.0)
            named = jnp.where(lane // 32 == (n // 2) % 4, named, 0.0)
            rank = nn(named.astype(BF), before)
            taken = (named > 0.5) & (rank == (n % 2).astype(F32))
            pick[a, aligned(q, 128)] = jnp.where(taken, 1.0, 0.0).astype(BF)
            pickw[a, aligned(q, 128)] = jnp.where(taken, weight, 0.0).astype(BF)
            return carry
        lax.fori_loop(0, 4, slots, 0)

    def to_plane(a, src, dst, phase):
        sem = phase * 3 + a
        spot = dst.at[aligned(plane[a], 16)]

        def send(j, carry):
            t = (plane[a] + j) % 32
            pltpu.make_async_remote_copy(
                src.at[aligned(t, 16)], spot, send_sem.at[sem], recv_sem.at[sem],
                device_id=device(a, line[a], t // 8, (t // 2) % 4, t % 2), device_id_type=MESH,
            ).start()
            return carry
        lax.fori_loop(1, 32, send, 0)
        pltpu.make_async_copy(src.at[aligned(plane[a], 16)], spot, recv_sem.at[sem]).start()

    for phase, chosen, rows, out, into in ((3, pick, tx, sx, rx), (4, pickw, tg, sd, rd)):
        for a in range(3):
            wait_bytes(rows[a], recv_sem.at[(phase - 2) * 3 + a])

            def gather(q, carry, a=a, chosen=chosen, rows=rows, out=out):
                out[a][aligned(q, 128)] = nn(chosen[a, aligned(q, 128)], rows[a][...]).astype(BF)
                return carry
            lax.fori_loop(0, 4, gather, 0)
            to_plane(a, out[a], into[a], phase)

    def reorder(got, phase):
        for a in range(3):
            wait_bytes(got[a], recv_sem.at[phase * 3 + a])

            def turn(q, carry, a=a):
                xc[aligned(q, 128), COLS[a][0]:COLS[a][1]] = nn(perm[a, aligned(q, 128)], got[a][...]).astype(BF)
                return carry
            lax.fori_loop(0, 4, turn, 0)

    reorder(rx, 3)
    for n in range(4):
        loads[n].wait()

    def first(i, carry):
        rows = aligned(i, 256)
        a_gate = nn(xc[rows], wg[i])
        a_up = nn(xc[rows], wu[i])
        sig = jax.nn.sigmoid(a_gate)
        active = a_gate * sig
        fa[rows] = active
        fb[rows] = a_up * sig * (1.0 + a_gate * (1.0 - sig))
        hid[rows] = (active * a_up).astype(BF)
        right[rows] = nt(hid[rows], pi[i])
        return carry
    lax.fori_loop(0, 2, first, 0)

    reorder(rd, 4)
    for n in range(4, 7):
        loads[n].wait()

    def second(i, carry):
        rows = aligned(i, 256)
        d_hidden = nt(xc[rows], wd[i])
        gu[rows] = (d_hidden * fa[rows]).astype(BF)
        gg[rows] = (d_hidden * fb[rows]).astype(BF)
        return carry
    lax.fori_loop(0, 2, second, 0)

    for a in range(3):
        cols = slice(*COLS[a])

        def third(i, carry, cols=cols):
            rows = aligned(i, 256)
            gc[rows, cols] = (nt(gg[rows], wg[i, cols]) + nt(gu[rows], wu[i, cols])).astype(BF)
            return carry
        lax.fori_loop(0, 2, third, 0)
        for q in range(4):
            gs[a][q * 128:q * 128 + 128] = tn(perm[a, :, q * 128:q * 128 + 128], gc[:, cols]).astype(BF)
        to_plane(a, gs[a], gr[a], 5)

    def fourth(i, carry):
        rows = aligned(i, 256)
        left = nt(xc[rows], po[i])
        low = lax.broadcasted_iota(jnp.int32, (256, 128), 1) < 64
        twice = right[rows]
        for j in range(32):
            spread = jnp.where(low, left[:, 2 * j:2 * j + 1], left[:, 2 * j + 1:2 * j + 2])
            outer[:, 128 * j:128 * j + 128] = (spread * twice).astype(BF)
        scc[rows] = nn(outer[...], tr[i]).astype(BF)
        return carry
    lax.fori_loop(0, 2, fourth, 0)
    for a in range(2):
        for q in range(4):
            ss[a][q * 128:q * 128 + 128] = tn(
                perm[a, :, q * 128:q * 128 + 128], scc[:, SCOLS[a][0]:SCOLS[a][1]]
            ).astype(BF)
        to_plane(a, ss[a], sr[a], 6)

    def home(a, got, part, into, phase):
        wait_bytes(got, recv_sem.at[phase * 3 + a])
        part[...] = tn(pick[a], got[...]).astype(BF)
        spot = into.at[aligned(line[a], 32)]
        on_line(a, lambda there: part.at[aligned(there, 32)], spot, phase + 2)
        pltpu.make_async_copy(part.at[aligned(line[a], 32)], spot, recv_sem.at[(phase + 2) * 3 + a]).start()

    def total(ref):
        return (ref[0:32].astype(F32) + ref[32:64].astype(F32)) + (ref[64:96].astype(F32) + ref[96:128].astype(F32))

    for a in range(3):
        home(a, gr[a], pg[a], hg[a], 5)
    for a in range(2):
        home(a, sr[a], pq[a], hq[a], 6)
    for a in range(3):
        wait_bytes(hg[a], recv_sem.at[7 * 3 + a])
        grads_out[:, COLS[a][0]:COLS[a][1]] = total(hg[a]).astype(BF)
    query = jnp.where(
        lax.broadcasted_iota(jnp.int32, (8, 32), 0) == jnp.broadcast_to(qid_ref[...], (8, 32)), 1.0, 0.0
    ).astype(F32)
    for a in range(2):
        wait_bytes(hq[a], recv_sem.at[8 * 3 + a])
        scores_out[:, SCOLS[a][0]:SCOLS[a][1]] = jnp.dot(
            query, total(hq[a]), precision=lax.Precision.HIGHEST, preferred_element_type=F32
        )
    for a in range(3):
        wait_bytes(meta.at[a, 0:3], send_sem.at[a])
        wait_bytes(tx[a].at[0:96], send_sem.at[3 + a])
        wait_bytes(tg[a].at[0:96], send_sem.at[6 + a])
        wait_bytes(sx[a].at[0:496], send_sem.at[9 + a])
        wait_bytes(sd[a].at[0:496], send_sem.at[12 + a])
        wait_bytes(gs[a].at[0:496], send_sem.at[15 + a])
        wait_bytes(pg[a].at[0:96], send_sem.at[21 + a])
    for a in range(2):
        wait_bytes(ss[a].at[0:496], send_sem.at[18 + a])
        wait_bytes(pq[a].at[0:96], send_sem.at[24 + a])


def body(tokens, out_grad, expert_ids, gate_w, query_ids, w_gate, w_up, w_down, proj_out, proj_in, train_grads):
    vmem = pl.BlockSpec(memory_space=pltpu.VMEM)
    hbm = pl.BlockSpec(memory_space=pl.ANY)

    def three(rows, dtype=BF):
        return [pltpu.VMEM((rows, w), dtype) for w in WIDTH]

    def two(rows):
        return [pltpu.VMEM((rows, s[1] - s[0]), BF) for s in SCOLS if s]

    scratch = [
        pltpu.VMEM((2, D, F), BF), pltpu.VMEM((2, D, F), BF), pltpu.VMEM((2, F, D), BF),
        pltpu.VMEM((2, 64, D), BF), pltpu.VMEM((2, 128, F), BF), pltpu.VMEM((2, 4096, TRAIN), BF),
        pltpu.VMEM((3, 4, 16, 128), BF), pltpu.VMEM((3, 512, 512), BF),
        pltpu.VMEM((3, 512, 128), BF), pltpu.VMEM((3, 512, 128), BF),
        *three(128), *three(128),
        *three(512), *three(512),
        *three(512), *three(512),
        pltpu.VMEM((512, D), BF), pltpu.VMEM((512, F), BF), pltpu.VMEM((512, F), F32), pltpu.VMEM((512, F), F32),
        pltpu.VMEM((512, 128), F32), pltpu.VMEM((512, F), BF), pltpu.VMEM((512, F), BF), pltpu.VMEM((512, D), BF),
        pltpu.VMEM((256, 4096), BF), pltpu.VMEM((512, TRAIN), BF),
        *three(512), *three(512),
        *two(512), *two(512),
        *three(128), *three(128), *two(128), *two(128),
        pltpu.SemaphoreType.DMA((7,)), pltpu.SemaphoreType.DMA((27,)), pltpu.SemaphoreType.DMA((27,)),
    ]
    return pl.pallas_call(
        kernel,
        out_shape=(jax.ShapeDtypeStruct((32, D), BF), jax.ShapeDtypeStruct((8, TRAIN), F32)),
        in_specs=[hbm, hbm, vmem, vmem, vmem] + [hbm] * 6,
        out_specs=(vmem, vmem),
        scratch_shapes=scratch,
        compiler_params=pltpu.CompilerParams(
            collective_id=0, has_side_effects=True, vmem_limit_bytes=60 * 1024 * 1024
        ),
        cost_estimate=pl.CostEstimate(flops=9_000_000_000, bytes_accessed=22_000_000, transcendentals=262_144),
    )(
        tokens, out_grad, expert_ids.T, gate_w.T, query_ids, w_gate, w_up, w_down,
        jnp.swapaxes(proj_out, 1, 2), jnp.swapaxes(proj_in, 1, 2), train_grads,
    )


def solution(mesh):
    rows = P(("group", "expert"), None)
    stack = P(("group", "expert"), None, None)
    return jax.shard_map(
        body,
        mesh=mesh,
        in_specs=(rows,) * 5 + (stack,) * 6,
        out_specs=(rows, rows),
        check_vma=False,
    )
```

```python
import jax
import jax.numpy as jnp
from jax import lax
from jax.experimental import pallas as pl
from jax.experimental.pallas import tpu as pltpu
from jax.sharding import PartitionSpec as P

MESH = pl.DeviceIdType.MESH
BF = jnp.bfloat16
F32 = jnp.float32
COLS = ((0, 640), (640, 1280), (1280, 2048))
SCOLS = ((0, 256), (256, 512), None)
WIDTH = tuple(b - a for a, b in COLS)
STEPS = {
    3: (((0, 384), (0, 384), (0, 384)), ((384, 640), (384, 640), (384, 768))),
    4: (((0, 384), (0, 384), (0, 384)), ((384, 640), (384, 640), (384, 768))),
    5: (((0, 256), (0, 256), (0, 256)), ((256, 512), (256, 512), (256, 512)), ((512, 640), (512, 640), (512, 768))),
    6: (((0, 256), (0, 256)),),
}
LOADS = ((0, 1, 2, 3), (4, 5, 6))
D = 2048
F = 512
TRAIN = 512


def nn(a, b):
    return jnp.dot(a, b, preferred_element_type=F32)


def nt(a, b):
    return lax.dot_general(a, b, (((1,), (1,)), ((), ())), preferred_element_type=F32)


def tn(a, b):
    return lax.dot_general(a, b, (((0,), (0,)), ((), ())), preferred_element_type=F32)


def coords(axis, line, u, v):
    return ((line, u, v), (u, line, v), (u, v, line))[axis]


def device(axis, line, u, v, core):
    y, z, x = coords(axis, line, u, v)
    return (y * 2 + core, z * 4 + x)


def expert_of(axis, line, u, v, core, which):
    group, place = device(axis, line, u, v, core)
    return group * 32 + place * 2 + which


def aligned(start, unit):
    return pl.ds(pl.multiple_of(start * unit, unit), unit)


def kernel(
    tok_h, og_h, ids_ref, gw_ref, qid_ref, wg_h, wu_h, wd_h, po_h, pi_h, tr_h,
    grads_out, scores_out,
    wg, wu, wd, po, pi, tr,
    tok, og, meta, perm, spread, pick, pickw,
    tx0, tx1, tx2, tg0, tg1, tg2,
    sx0, sx1, sx2, sd0, sd1, sd2,
    rx0, rx1, rx2, rd0, rd1, rd2,
    xc, hid, fa, fb, dh, right, gg, gu, gc, outer, scc,
    gs0, gs1, gs2, gr0, gr1, gr2,
    ss0, ss1, sr0, sr1,
    pg0, pg1, pg2, hg0, hg1, hg2, pq0, pq1, hq0, hq1,
    load_sem, send_sem, recv_sem,
):
    tx, tg = (tx0, tx1, tx2), (tg0, tg1, tg2)
    sx, sd = (sx0, sx1, sx2), (sd0, sd1, sd2)
    rx, rd = (rx0, rx1, rx2), (rd0, rd1, rd2)
    gs, gr = (gs0, gs1, gs2), (gr0, gr1, gr2)
    ss, sr = (ss0, ss1), (sr0, sr1)
    pg, hg = (pg0, pg1, pg2), (hg0, hg1, hg2)
    pq, hq = (pq0, pq1), (hq0, hq1)
    group, place = lax.axis_index("group"), lax.axis_index("expert")
    y, core = group // 2, group % 2
    z, x = place // 4, place % 4
    line = (y, z, x)
    uv = ((z, x), (y, x), (y, z))
    plane = tuple((u * 4 + v) * 2 + core for u, v in uv)

    loads = [
        pltpu.make_async_copy(src, dst, load_sem.at[n])
        for n, (src, dst) in enumerate(
            (
                (wg_h, wg), (wu_h, wu), (pi_h, pi.at[:, 0:64]), (pi_h, pi.at[:, 64:128]),
                (wd_h, wd), (po_h, po), (tr_h, tr),
            )
        )
    ]

    staged = [pltpu.make_async_copy(src, dst, load_sem.at[7 + n]) for n, (src, dst) in enumerate(((tok_h, tok), (og_h, og)))]
    for copy in staged:
        copy.start()
    barrier = pltpu.get_barrier_semaphore()
    for a in range(3):
        for d in range(1, 4):
            for c in range(2):
                pl.semaphore_signal(
                    barrier, inc=1, device_id=device(a, lax.rem(line[a] + d, 4), uv[a][0], uv[a][1], c), device_id_type=MESH
                )
    pl.semaphore_signal(barrier, inc=1, device_id=(y * 2 + 1 - core, place), device_id_type=MESH)

    own = jnp.concatenate([ids_ref[...].astype(F32), gw_ref[...].astype(F32)], axis=0).astype(BF)
    for a in range(3):
        lane = lax.broadcasted_iota(jnp.int32, (32, 128), 1)
        row = lax.broadcasted_iota(jnp.int32, (32, 128), 0)
        put = jnp.where(lane == row + 32 * line[a], 1.0, 0.0).astype(BF)
        meta[a, pl.ds(line[a], 1)] = nn(own, put).astype(BF)[None]
    pl.semaphore_wait(barrier, 19)

    def spot_of(phase, a, step=0):
        return (phase * 3 + a) * 3 + step

    def line_peers(a):
        for d in range(1, 4):
            there = lax.rem(line[a] + d, 4)
            yield there, device(a, there, uv[a][0], uv[a][1], core)

    def on_line(a, src_of, dst, phase):
        sem = spot_of(phase, a)
        for there, dev in line_peers(a):
            pltpu.make_async_remote_copy(
                src_of(there), dst, send_sem.at[sem], recv_sem.at[sem], device_id=dev, device_id_type=MESH
            ).start()

    def wait_bytes(ref, sem):
        pltpu.make_async_copy(ref, ref, sem).wait()

    for a in range(3):
        on_line(a, lambda there, a=a: meta.at[a, line[a]], meta.at[a, line[a]], 0)
    for n, (phase, src, dst) in enumerate(((1, tok, tx), (2, og, tg))):
        staged[n].wait()
        for a in range(3):
            part = src.at[:, COLS[a][0]:COLS[a][1]]
            spot = dst[a].at[aligned(line[a], 32)]
            on_line(a, lambda there, part=part: part, spot, phase)
            pltpu.make_async_copy(part, spot, recv_sem.at[spot_of(phase, a)]).start()

    r0 = lax.broadcasted_iota(jnp.int32, (128, 128), 0)
    c1 = lax.broadcasted_iota(jnp.int32, (128, 128), 1)
    before = jnp.where((r0 < c1) & ((r0 >> 5) == (c1 >> 5)), 1.0, 0.0).astype(BF)
    r1 = lax.broadcasted_iota(jnp.int32, (1, 8, 128), 1)
    c2 = lax.broadcasted_iota(jnp.int32, (1, 8, 128), 2)
    tile = jnp.where((c2 >> 5) == (r1 >> 1), (r1 & 1) + 1, -1).astype(F32)
    r2 = lax.broadcasted_iota(jnp.int32, (64, 128), 0)

    def choose(a):
        wait_bytes(meta.at[a, 0:3], recv_sem.at[spot_of(0, a)])
        both = (meta[a, 0].astype(F32) + meta[a, 1].astype(F32)) + (meta[a, 2].astype(F32) + meta[a, 3].astype(F32))
        wanted = expert_of(a, line[a], r2 >> 4, (r2 >> 2) & 3, (r2 >> 1) & 1, r2 & 1).astype(F32)
        named = jnp.zeros((64, 128), F32)
        weight = jnp.zeros((64, 128), F32)
        for k in range(8):
            hit = both[k:k + 1, :] == wanted
            named = named + jnp.where(hit, 1.0, 0.0)
            weight = weight + jnp.where(hit, both[8 + k:9 + k, :], 0.0)
        code = named * (nn(named.astype(BF), before) + 1.0)
        taken = jnp.broadcast_to(code[:, None, :], (64, 8, 128)) == tile
        pick[a] = jnp.where(taken, 1.0, 0.0).reshape(512, 128).astype(BF)
        pickw[a] = jnp.where(taken, jnp.broadcast_to(weight[:, None, :], (64, 8, 128)), 0.0).reshape(512, 128).astype(BF)

    def sender(a, src, dst, phase, step):
        sem = spot_of(phase, a, step)
        cols = STEPS[phase][step][a]
        cols = slice(*cols)
        spot = dst.at[aligned(plane[a], 16), cols]

        def send(du, dv, flip):
            u = lax.rem(uv[a][0] + du, 4)
            v = lax.rem(uv[a][1] + dv, 4)
            c = 1 - core if flip else core
            pltpu.make_async_remote_copy(
                src.at[aligned((u * 4 + v) * 2 + c, 16), cols], spot, send_sem.at[sem], recv_sem.at[sem],
                device_id=device(a, line[a], u, v, c), device_id_type=MESH,
            ).start()

        return send, lambda: pltpu.make_async_copy(src.at[aligned(plane[a], 16), cols], spot, recv_sem.at[sem]).start()

    def to_planes(jobs):
        made = [sender(*job) for job in jobs]

        def ahead(d, carry):
            for dv in range(4):
                for flip in range(2):
                    for send, _ in made:
                        send(d, dv, flip)
            return carry
        lax.fori_loop(1, 4, ahead, 0)
        for dv in range(1, 4):
            for flip in range(2):
                for send, _ in made:
                    send(0, dv, flip)
        for send, keep in made:
            send(0, 0, 1)
            keep()

    for a in range(3):
        choose(a)
    for phase, chosen, rows, out, into in ((3, pick, tx, sx, rx), (4, pickw, tg, sd, rd)):
        for step, ranges in enumerate(STEPS[phase]):
            for a in range(3):
                if step == 0:
                    wait_bytes(rows[a], recv_sem.at[spot_of(phase - 2, a)])
                cols = slice(*ranges[a])
                for q in range(2):
                    span = slice(q * 256, q * 256 + 256)
                    out[a][span, cols] = nn(chosen[a, span], rows[a][:, cols]).astype(BF)
            to_planes([(a, out[a], into[a], phase, step) for a in range(3)])
        for n in LOADS[phase - 3]:
            loads[n].start()

    for a in range(3):
        for q in range(2):
            n = lax.broadcasted_iota(jnp.int32, (128, 256), 0) + q * 128
            lane = lax.broadcasted_iota(jnp.int32, (128, 256), 1)
            l0, u0, v0 = (
                (n >> 6, (n >> 4) & 3, (n >> 2) & 3), ((n >> 4) & 3, n >> 6, (n >> 2) & 3), ((n >> 2) & 3, n >> 6, (n >> 4) & 3)
            )[a]
            at = ((u0 * 4 + v0) * 2 + ((n >> 1) & 1)) * 8 + l0 * 2 + (n & 1)
            perm[a, q * 128:q * 128 + 128] = jnp.where(lane == at, 1.0, 0.0).astype(BF)
    for q in range(8):
        n = lax.broadcasted_iota(jnp.int32, (128, 512), 0)
        lane = lax.broadcasted_iota(jnp.int32, (128, 512), 1) + q * 512
        spread[:, q * 512:q * 512 + 512] = jnp.where((lane >> 6) == (n & 63), 1.0, 0.0).astype(BF)

    def reorder(got, phase, step):
        for a in range(3):
            start, stop = STEPS[phase][step][a]
            wait_bytes(got[a].at[:, start:stop], recv_sem.at[spot_of(phase, a, step)])
            for k in range(start, stop, 128):
                units = got[a][:, k:k + 128].astype(F32).reshape(32, 2, 8, 128)
                for i in range(2):
                    xc[i * 256:i * 256 + 256, COLS[a][0] + k:COLS[a][0] + k + 128] = nn(
                        perm[a], units[:, i].reshape(256, 128).astype(BF)
                    ).astype(BF)

    def restore(a, rows, out):
        for k in range(0, out.shape[1], 128):
            both = [
                tn(perm[a], rows[i * 256:i * 256 + 256, k:k + 128]).reshape(32, 1, 8, 128) for i in range(2)
            ]
            out[:, k:k + 128] = jnp.concatenate(both, axis=1).reshape(512, 128).astype(BF)

    for step in range(len(STEPS[3])):
        reorder(rx, 3, step)
    for n in range(4):
        loads[n].wait()

    def first(i, carry):
        rows = aligned(i, 256)
        a_gate = nn(xc[rows], wg[i])
        a_up = nn(xc[rows], wu[i])
        sig = jax.nn.sigmoid(a_gate)
        active = a_gate * sig
        fa[rows] = active
        fb[rows] = a_up * sig * (1.0 + a_gate * (1.0 - sig))
        hid[rows] = (active * a_up).astype(BF)
        right[rows] = nt(hid[rows], pi[i])
        return carry
    lax.fori_loop(0, 2, first, 0)

    for n in range(4, 7):
        loads[n].wait()
    for step, ranges in enumerate(STEPS[4]):
        reorder(rd, 4, step)
        for i in range(2):
            rows = slice(i * 256, i * 256 + 256)
            d_hidden = dh[rows] if step else None
            for a in range(3):
                cols = slice(COLS[a][0] + ranges[a][0], COLS[a][0] + ranges[a][1])
                term = nt(xc[rows, cols], wd[i, :, cols])
                d_hidden = term if d_hidden is None else d_hidden + term
            if step < len(STEPS[4]) - 1:
                dh[rows] = d_hidden
            else:
                gu[rows] = (d_hidden * fa[rows]).astype(BF)
                gg[rows] = (d_hidden * fb[rows]).astype(BF)

    for step, ranges in enumerate(STEPS[5]):
        for a in range(3):
            cols = slice(COLS[a][0] + ranges[a][0], COLS[a][0] + ranges[a][1])
            for i in range(2):
                rows = slice(i * 256, i * 256 + 256)
                gc[rows, cols] = (nt(gg[rows], wg[i, cols]) + nt(gu[rows], wu[i, cols])).astype(BF)
            restore(a, gc.at[:, cols], gs[a].at[:, slice(*ranges[a])])
        to_planes([(a, gs[a], gr[a], 5, step) for a in range(3)])

    for i in range(2):
        rows = slice(i * 256, i * 256 + 256)
        left = nt(xc[rows], po[i])
        high = left.astype(BF)
        terms = jnp.concatenate([high, (left - high.astype(F32)).astype(BF)], axis=1)
        twice = right[rows]
        for j in range(8):
            wide = nn(terms, spread[:, 512 * j:512 * j + 512])
            for m in range(4):
                at = 512 * j + 128 * m
                outer[:, at:at + 128] = (wide[:, 128 * m:128 * m + 128] * twice).astype(BF)
        scc[rows] = nn(outer[...], tr[i]).astype(BF)
    for a in range(2):
        restore(a, scc.at[:, SCOLS[a][0]:SCOLS[a][1]], ss[a])
    to_planes([(a, ss[a], sr[a], 6, 0) for a in range(2)])

    def home(parts, got, part, into, phase):
        for step, ranges in enumerate(STEPS[phase]):
            for a in parts:
                cols = slice(*ranges[a])
                wait_bytes(got[a].at[:, cols], recv_sem.at[spot_of(phase, a, step)])
                part[a][:, cols] = tn(pick[a], got[a][:, cols]).astype(BF)
        for a in parts:
            spot = into[a].at[aligned(line[a], 32)]
            on_line(a, lambda there, a=a: part[a].at[aligned(there, 32)], spot, phase + 2)
            pltpu.make_async_copy(
                part[a].at[aligned(line[a], 32)], spot, recv_sem.at[spot_of(phase + 2, a)]
            ).start()

    def total(ref):
        return (ref[0:32].astype(F32) + ref[32:64].astype(F32)) + (ref[64:96].astype(F32) + ref[96:128].astype(F32))

    home(range(3), gr, pg, hg, 5)
    home(range(2), sr, pq, hq, 6)
    for a in range(3):
        wait_bytes(hg[a], recv_sem.at[spot_of(7, a)])
        grads_out[:, COLS[a][0]:COLS[a][1]] = total(hg[a]).astype(BF)
    query = jnp.where(
        lax.broadcasted_iota(jnp.int32, (8, 32), 0) == jnp.broadcast_to(qid_ref[...], (8, 32)), 1.0, 0.0
    ).astype(F32)
    for a in range(2):
        wait_bytes(hq[a], recv_sem.at[spot_of(8, a)])
        scores_out[:, SCOLS[a][0]:SCOLS[a][1]] = jnp.dot(
            query, total(hq[a]), precision=lax.Precision.HIGHEST, preferred_element_type=F32
        )
    for a in range(3):
        wait_bytes(meta.at[a, 0:3], send_sem.at[spot_of(0, a)])
        wait_bytes(tx[a].at[0:96], send_sem.at[spot_of(1, a)])
        wait_bytes(tg[a].at[0:96], send_sem.at[spot_of(2, a)])
        wait_bytes(pg[a].at[0:96], send_sem.at[spot_of(7, a)])
        for phase, sent in ((3, sx), (4, sd), (5, gs)):
            for step, ranges in enumerate(STEPS[phase]):
                wait_bytes(sent[a].at[0:496, slice(*ranges[a])], send_sem.at[spot_of(phase, a, step)])
    for a in range(2):
        wait_bytes(ss[a].at[0:496], send_sem.at[spot_of(6, a)])
        wait_bytes(pq[a].at[0:96], send_sem.at[spot_of(8, a)])


def hand_over(grads, scores, grads_out, scores_out):
    grads_out[...] = grads[...]
    scores_out[...] = scores[...]


def body(tokens, out_grad, expert_ids, gate_w, query_ids, w_gate, w_up, w_down, proj_out, proj_in, train_grads):
    vmem = pl.BlockSpec(memory_space=pltpu.VMEM)
    hbm = pl.BlockSpec(memory_space=pl.ANY)

    def three(rows, dtype=BF):
        return [pltpu.VMEM((rows, w), dtype) for w in WIDTH]

    def two(rows):
        return [pltpu.VMEM((rows, s[1] - s[0]), BF) for s in SCOLS if s]

    scratch = [
        pltpu.VMEM((2, D, F), BF), pltpu.VMEM((2, D, F), BF), pltpu.VMEM((2, F, D), BF),
        pltpu.VMEM((2, 64, D), BF), pltpu.VMEM((2, 128, F), BF), pltpu.VMEM((2, 4096, TRAIN), BF),
        pltpu.VMEM((32, D), BF), pltpu.VMEM((32, D), BF), pltpu.VMEM((3, 4, 16, 128), BF), pltpu.VMEM((3, 256, 256), BF), pltpu.VMEM((128, 4096), BF),
        pltpu.VMEM((3, 512, 128), BF), pltpu.VMEM((3, 512, 128), BF),
        *three(128), *three(128),
        *three(512), *three(512),
        *three(512), *three(512),
        pltpu.VMEM((512, D), BF), pltpu.VMEM((512, F), BF), pltpu.VMEM((512, F), F32), pltpu.VMEM((512, F), F32),
        pltpu.VMEM((512, F), F32),
        pltpu.VMEM((512, 128), F32), pltpu.VMEM((512, F), BF), pltpu.VMEM((512, F), BF), pltpu.VMEM((512, D), BF),
        pltpu.VMEM((256, 4096), BF), pltpu.VMEM((512, TRAIN), BF),
        *three(512), *three(512),
        *two(512), *two(512),
        *three(128), *three(128), *two(128), *two(128),
        pltpu.SemaphoreType.DMA((9,)), pltpu.SemaphoreType.DMA((81,)), pltpu.SemaphoreType.DMA((81,)),
    ]
    done = pl.pallas_call(
        kernel,
        out_shape=(jax.ShapeDtypeStruct((32, D), BF), jax.ShapeDtypeStruct((8, TRAIN), F32)),
        in_specs=[hbm, hbm, vmem, vmem, vmem] + [hbm] * 6,
        out_specs=(vmem, vmem),
        scratch_shapes=scratch,
        compiler_params=pltpu.CompilerParams(
            collective_id=0, has_side_effects=True, vmem_limit_bytes=60 * 1024 * 1024
        ),
        cost_estimate=pl.CostEstimate(flops=9_000_000_000, bytes_accessed=22_000_000, transcendentals=262_144),
    )(
        tokens, out_grad, expert_ids.T, gate_w.T, query_ids, w_gate, w_up, w_down,
        jnp.swapaxes(proj_out, 1, 2), jnp.swapaxes(proj_in, 1, 2), train_grads,
    )
    return pl.pallas_call(
        hand_over,
        out_shape=(jax.ShapeDtypeStruct((32, D), BF), jax.ShapeDtypeStruct((8, TRAIN), F32)),
        in_specs=[vmem, vmem],
        out_specs=(vmem, vmem),
    )(*done)


def solution(mesh):
    rows = P(("group", "expert"), None)
    stack = P(("group", "expert"), None, None)
    return jax.shard_map(
        body,
        mesh=mesh,
        in_specs=(rows,) * 5 + (stack,) * 6,
        out_specs=(rows, rows),
        check_vma=False,
    )
```

```python
import jax
import jax.numpy as jnp
from jax import lax
from jax.experimental import pallas as pl
from jax.experimental.pallas import tpu as pltpu
from jax.sharding import PartitionSpec as P

MESH = pl.DeviceIdType.MESH
BF = jnp.bfloat16
F32 = jnp.float32
COLS = ((0, 640), (640, 1280), (1280, 2048))
SCOLS = ((0, 256), (256, 512), None)
WIDTH = tuple(b - a for a, b in COLS)
STEPS = {
    3: (((0, 384), (0, 384), (0, 384)), ((384, 640), (384, 640), (384, 768))),
    4: (((0, 384), (0, 384), (0, 384)), ((384, 640), (384, 640), (384, 768))),
    5: (((0, 128), (0, 128), (0, 128)), ((128, 384), (128, 384), (128, 384)), ((384, 640), (384, 640), (384, 768))),
    6: (((0, 256), (0, 256)),),
}
LOADS = ((0, 1, 2, 3), (4, 5, 6))
D = 2048
F = 512
TRAIN = 512


def nn(a, b):
    return jnp.dot(a, b, preferred_element_type=F32)


def nt(a, b):
    return lax.dot_general(a, b, (((1,), (1,)), ((), ())), preferred_element_type=F32)


def tn(a, b):
    return lax.dot_general(a, b, (((0,), (0,)), ((), ())), preferred_element_type=F32)


def coords(axis, line, u, v):
    return ((line, u, v), (u, line, v), (u, v, line))[axis]


def device(axis, line, u, v, core):
    y, z, x = coords(axis, line, u, v)
    return (y * 2 + core, z * 4 + x)


def expert_of(axis, line, u, v, core, which):
    group, place = device(axis, line, u, v, core)
    return group * 32 + place * 2 + which


def aligned(start, unit):
    return pl.ds(pl.multiple_of(start * unit, unit), unit)


def kernel(
    tok_h, og_h, ids_ref, gw_ref, wg_h, wu_h, wd_h, po_h, pi_h, tr_h,
    hg0, hg1, hg2, hq0, hq1,
    wg, wu, wd, po, pi, tr,
    tok, og, meta, perm, spread, pick, pickw,
    tx0, tx1, tx2, tg0, tg1, tg2,
    sx0, sx1, sx2, sd0, sd1, sd2,
    rx0, rx1, rx2, rd0, rd1, rd2,
    xc, hid, fa, fb, dh, right, gg, gu, gc, outer, scc,
    gs0, gs1, gs2, gr0, gr1, gr2,
    ss0, ss1, sr0, sr1,
    pg0, pg1, pg2, pq0, pq1,
    load_sem, send_sem, recv_sem,
):
    tx, tg = (tx0, tx1, tx2), (tg0, tg1, tg2)
    sx, sd = (sx0, sx1, sx2), (sd0, sd1, sd2)
    rx, rd = (rx0, rx1, rx2), (rd0, rd1, rd2)
    gs, gr = (gs0, gs1, gs2), (gr0, gr1, gr2)
    ss, sr = (ss0, ss1), (sr0, sr1)
    pg, hg = (pg0, pg1, pg2), (hg0, hg1, hg2)
    pq, hq = (pq0, pq1), (hq0, hq1)
    group, place = lax.axis_index("group"), lax.axis_index("expert")
    y, core = group // 2, group % 2
    z, x = place // 4, place % 4
    line = (y, z, x)
    uv = ((z, x), (y, x), (y, z))
    plane = tuple((u * 4 + v) * 2 + core for u, v in uv)

    loads = [
        pltpu.make_async_copy(src, dst, load_sem.at[n])
        for n, (src, dst) in enumerate(
            (
                (wg_h, wg), (wu_h, wu), (pi_h, pi.at[:, 0:64]), (pi_h, pi.at[:, 64:128]),
                (wd_h, wd), (po_h, po), (tr_h, tr),
            )
        )
    ]

    staged = [pltpu.make_async_copy(src, dst, load_sem.at[7 + n]) for n, (src, dst) in enumerate(((tok_h, tok), (og_h, og)))]
    for copy in staged:
        copy.start()
    barrier = pltpu.get_barrier_semaphore()
    for a in range(3):
        for d in range(1, 4):
            for c in range(2):
                pl.semaphore_signal(
                    barrier, inc=1, device_id=device(a, lax.rem(line[a] + d, 4), uv[a][0], uv[a][1], c), device_id_type=MESH
                )
    pl.semaphore_signal(barrier, inc=1, device_id=(y * 2 + 1 - core, place), device_id_type=MESH)

    own = jnp.concatenate([ids_ref[...].astype(F32), gw_ref[...].astype(F32)], axis=0).astype(BF)
    for a in range(3):
        lane = lax.broadcasted_iota(jnp.int32, (32, 128), 1)
        row = lax.broadcasted_iota(jnp.int32, (32, 128), 0)
        put = jnp.where(lane == row + 32 * line[a], 1.0, 0.0).astype(BF)
        meta[a, pl.ds(line[a], 1)] = nn(own, put).astype(BF)[None]
    pl.semaphore_wait(barrier, 19)

    def spot_of(phase, a, step=0):
        return (phase * 3 + a) * 3 + step

    def line_peers(a):
        for d in range(1, 4):
            there = lax.rem(line[a] + d, 4)
            yield there, device(a, there, uv[a][0], uv[a][1], core)

    def on_line(a, src_of, dst, phase):
        sem = spot_of(phase, a)
        for there, dev in line_peers(a):
            pltpu.make_async_remote_copy(
                src_of(there), dst, send_sem.at[sem], recv_sem.at[sem], device_id=dev, device_id_type=MESH
            ).start()

    def wait_bytes(ref, sem):
        pltpu.make_async_copy(ref, ref, sem).wait()

    for a in range(3):
        on_line(a, lambda there, a=a: meta.at[a, line[a]], meta.at[a, line[a]], 0)
    for n, (phase, src, dst) in enumerate(((1, tok, tx), (2, og, tg))):
        staged[n].wait()
        for a in range(3):
            part = src.at[:, COLS[a][0]:COLS[a][1]]
            spot = dst[a].at[aligned(line[a], 32)]
            on_line(a, lambda there, part=part: part, spot, phase)
            pltpu.make_async_copy(part, spot, recv_sem.at[spot_of(phase, a)]).start()

    r0 = lax.broadcasted_iota(jnp.int32, (128, 128), 0)
    c1 = lax.broadcasted_iota(jnp.int32, (128, 128), 1)
    before = jnp.where((r0 < c1) & ((r0 >> 5) == (c1 >> 5)), 1.0, 0.0).astype(BF)
    r1 = lax.broadcasted_iota(jnp.int32, (1, 8, 128), 1)
    c2 = lax.broadcasted_iota(jnp.int32, (1, 8, 128), 2)
    tile = jnp.where((c2 >> 5) == (r1 >> 1), (r1 & 1) + 1, -1).astype(F32)
    r2 = lax.broadcasted_iota(jnp.int32, (64, 128), 0)

    def choose(a):
        wait_bytes(meta.at[a, 0:3], recv_sem.at[spot_of(0, a)])
        both = (meta[a, 0].astype(F32) + meta[a, 1].astype(F32)) + (meta[a, 2].astype(F32) + meta[a, 3].astype(F32))
        wanted = expert_of(a, line[a], r2 >> 4, (r2 >> 2) & 3, (r2 >> 1) & 1, r2 & 1).astype(F32)
        named = jnp.zeros((64, 128), F32)
        weight = jnp.zeros((64, 128), F32)
        for k in range(8):
            hit = both[k:k + 1, :] == wanted
            named = named + jnp.where(hit, 1.0, 0.0)
            weight = weight + jnp.where(hit, both[8 + k:9 + k, :], 0.0)
        code = named * (nn(named.astype(BF), before) + 1.0)
        taken = jnp.broadcast_to(code[:, None, :], (64, 8, 128)) == tile
        pick[a] = jnp.where(taken, 1.0, 0.0).reshape(512, 128).astype(BF)
        pickw[a] = jnp.where(taken, jnp.broadcast_to(weight[:, None, :], (64, 8, 128)), 0.0).reshape(512, 128).astype(BF)

    def sender(a, src, dst, phase, step):
        sem = spot_of(phase, a, step)
        cols = STEPS[phase][step][a]
        cols = slice(*cols)
        spot = dst.at[aligned(plane[a], 16), cols]

        def send(du, dv, flip):
            u = lax.rem(uv[a][0] + du, 4)
            v = lax.rem(uv[a][1] + dv, 4)
            c = 1 - core if flip else core
            pltpu.make_async_remote_copy(
                src.at[aligned((u * 4 + v) * 2 + c, 16), cols], spot, send_sem.at[sem], recv_sem.at[sem],
                device_id=device(a, line[a], u, v, c), device_id_type=MESH,
            ).start()

        return send, lambda: pltpu.make_async_copy(src.at[aligned(plane[a], 16), cols], spot, recv_sem.at[sem]).start()

    def to_planes(jobs):
        made = [sender(*job) for job in jobs]

        def row(du):
            for dv in (2, 1, 3, 0):
                for flip in range(2):
                    for send, _ in made:
                        send(du, dv, flip)

        def ahead(d, carry):
            row(d)
            return carry
        lax.fori_loop(2, 4, ahead, 0)
        row(1)
        for dv in (2, 1, 3):
            for flip in range(2):
                for send, _ in made:
                    send(0, dv, flip)
        for send, keep in made:
            send(0, 0, 1)
            keep()

    for a in range(3):
        choose(a)
    for phase, chosen, rows, out, into in ((3, pick, tx, sx, rx), (4, pickw, tg, sd, rd)):
        for step, ranges in enumerate(STEPS[phase]):
            for a in range(3):
                if step == 0:
                    wait_bytes(rows[a], recv_sem.at[spot_of(phase - 2, a)])
                cols = slice(*ranges[a])
                for q in range(2):
                    span = slice(q * 256, q * 256 + 256)
                    out[a][span, cols] = nn(chosen[a, span], rows[a][:, cols]).astype(BF)
            to_planes([(a, out[a], into[a], phase, step) for a in range(3)])
        for n in LOADS[phase - 3]:
            loads[n].start()

    for a in range(3):
        for q in range(2):
            n = lax.broadcasted_iota(jnp.int32, (128, 256), 0) + q * 128
            lane = lax.broadcasted_iota(jnp.int32, (128, 256), 1)
            l0, u0, v0 = (
                (n >> 6, (n >> 4) & 3, (n >> 2) & 3), ((n >> 4) & 3, n >> 6, (n >> 2) & 3), ((n >> 2) & 3, n >> 6, (n >> 4) & 3)
            )[a]
            at = ((u0 * 4 + v0) * 2 + ((n >> 1) & 1)) * 8 + l0 * 2 + (n & 1)
            perm[a, q * 128:q * 128 + 128] = jnp.where(lane == at, 1.0, 0.0).astype(BF)
    for q in range(8):
        n = lax.broadcasted_iota(jnp.int32, (128, 512), 0)
        lane = lax.broadcasted_iota(jnp.int32, (128, 512), 1) + q * 512
        spread[:, q * 512:q * 512 + 512] = jnp.where((lane >> 6) == (n & 63), 1.0, 0.0).astype(BF)

    def reorder(got, phase, step):
        for a in range(3):
            start, stop = STEPS[phase][step][a]
            wait_bytes(got[a].at[:, start:stop], recv_sem.at[spot_of(phase, a, step)])
            for k in range(start, stop, 128):
                units = got[a][:, k:k + 128].astype(F32).reshape(32, 2, 8, 128)
                for i in range(2):
                    xc[i * 256:i * 256 + 256, COLS[a][0] + k:COLS[a][0] + k + 128] = nn(
                        perm[a], units[:, i].reshape(256, 128).astype(BF)
                    ).astype(BF)

    def restore(a, rows, out):
        for k in range(0, out.shape[1], 128):
            both = [
                tn(perm[a], rows[i * 256:i * 256 + 256, k:k + 128]).reshape(32, 1, 8, 128) for i in range(2)
            ]
            out[:, k:k + 128] = jnp.concatenate(both, axis=1).reshape(512, 128).astype(BF)

    for step in range(len(STEPS[3])):
        reorder(rx, 3, step)
    for n in range(4):
        loads[n].wait()

    def first(i, carry):
        rows = aligned(i, 256)
        a_gate = nn(xc[rows], wg[i])
        a_up = nn(xc[rows], wu[i])
        sig = jax.nn.sigmoid(a_gate)
        active = a_gate * sig
        fa[rows] = active
        fb[rows] = a_up * sig * (1.0 + a_gate * (1.0 - sig))
        hid[rows] = (active * a_up).astype(BF)
        right[rows] = nt(hid[rows], pi[i])
        return carry
    lax.fori_loop(0, 2, first, 0)

    for n in range(4, 7):
        loads[n].wait()
    for step, ranges in enumerate(STEPS[4]):
        reorder(rd, 4, step)
        for i in range(2):
            rows = slice(i * 256, i * 256 + 256)
            d_hidden = dh[rows] if step else None
            for a in range(3):
                cols = slice(COLS[a][0] + ranges[a][0], COLS[a][0] + ranges[a][1])
                term = nt(xc[rows, cols], wd[i, :, cols])
                d_hidden = term if d_hidden is None else d_hidden + term
            if step < len(STEPS[4]) - 1:
                dh[rows] = d_hidden
            else:
                gu[rows] = (d_hidden * fa[rows]).astype(BF)
                gg[rows] = (d_hidden * fb[rows]).astype(BF)

    for step, ranges in enumerate(STEPS[5]):
        for a in range(3):
            cols = slice(COLS[a][0] + ranges[a][0], COLS[a][0] + ranges[a][1])
            for i in range(2):
                rows = slice(i * 256, i * 256 + 256)
                gc[rows, cols] = (nt(gg[rows], wg[i, cols]) + nt(gu[rows], wu[i, cols])).astype(BF)
            restore(a, gc.at[:, cols], gs[a].at[:, slice(*ranges[a])])
        to_planes([(a, gs[a], gr[a], 5, step) for a in range(3)])

    for i in range(2):
        rows = slice(i * 256, i * 256 + 256)
        left = nt(xc[rows], po[i])
        high = left.astype(BF)
        terms = jnp.concatenate([high, (left - high.astype(F32)).astype(BF)], axis=1)
        twice = right[rows]
        for j in range(8):
            wide = nn(terms, spread[:, 512 * j:512 * j + 512])
            for m in range(4):
                at = 512 * j + 128 * m
                outer[:, at:at + 128] = (wide[:, 128 * m:128 * m + 128] * twice).astype(BF)
        scc[rows] = nn(outer[...], tr[i]).astype(BF)
    for a in range(2):
        restore(a, scc.at[:, SCOLS[a][0]:SCOLS[a][1]], ss[a])
    to_planes([(a, ss[a], sr[a], 6, 0) for a in range(2)])

    def home(parts, got, part, into, phase):
        for step, ranges in enumerate(STEPS[phase]):
            for a in parts:
                cols = slice(*ranges[a])
                wait_bytes(got[a].at[:, cols], recv_sem.at[spot_of(phase, a, step)])
                part[a][:, cols] = tn(pick[a], got[a][:, cols]).astype(BF)
        for a in parts:
            spot = into[a].at[aligned(line[a], 32)]
            on_line(a, lambda there, a=a: part[a].at[aligned(there, 32)], spot, phase + 2)
            pltpu.make_async_copy(
                part[a].at[aligned(line[a], 32)], spot, recv_sem.at[spot_of(phase + 2, a)]
            ).start()

    home(range(3), gr, pg, hg, 5)
    home(range(2), sr, pq, hq, 6)
    for a in range(3):
        wait_bytes(hg[a], recv_sem.at[spot_of(7, a)])
    for a in range(2):
        wait_bytes(hq[a], recv_sem.at[spot_of(8, a)])
    for a in range(3):
        wait_bytes(meta.at[a, 0:3], send_sem.at[spot_of(0, a)])
        wait_bytes(tx[a].at[0:96], send_sem.at[spot_of(1, a)])
        wait_bytes(tg[a].at[0:96], send_sem.at[spot_of(2, a)])
        wait_bytes(pg[a].at[0:96], send_sem.at[spot_of(7, a)])
        for phase, sent in ((3, sx), (4, sd), (5, gs)):
            for step, ranges in enumerate(STEPS[phase]):
                wait_bytes(sent[a].at[0:496, slice(*ranges[a])], send_sem.at[spot_of(phase, a, step)])
    for a in range(2):
        wait_bytes(ss[a].at[0:496], send_sem.at[spot_of(6, a)])
        wait_bytes(pq[a].at[0:96], send_sem.at[spot_of(8, a)])


def close(hg0, hg1, hg2, hq0, hq1, qid_ref, grads_out, scores_out):
    def total(ref):
        return (ref[0:32].astype(F32) + ref[32:64].astype(F32)) + (ref[64:96].astype(F32) + ref[96:128].astype(F32))

    for a, ref in enumerate((hg0, hg1, hg2)):
        grads_out[:, COLS[a][0]:COLS[a][1]] = total(ref).astype(BF)
    query = jnp.where(
        lax.broadcasted_iota(jnp.int32, (8, 32), 0) == jnp.broadcast_to(qid_ref[...], (8, 32)), 1.0, 0.0
    ).astype(F32)
    for a, ref in enumerate((hq0, hq1)):
        scores_out[:, SCOLS[a][0]:SCOLS[a][1]] = jnp.dot(
            query, total(ref), precision=lax.Precision.HIGHEST, preferred_element_type=F32
        )


def body(tokens, out_grad, expert_ids, gate_w, query_ids, w_gate, w_up, w_down, proj_out, proj_in, train_grads):
    vmem = pl.BlockSpec(memory_space=pltpu.VMEM)
    hbm = pl.BlockSpec(memory_space=pl.ANY)

    def three(rows, dtype=BF):
        return [pltpu.VMEM((rows, w), dtype) for w in WIDTH]

    def two(rows):
        return [pltpu.VMEM((rows, s[1] - s[0]), BF) for s in SCOLS if s]

    scratch = [
        pltpu.VMEM((2, D, F), BF), pltpu.VMEM((2, D, F), BF), pltpu.VMEM((2, F, D), BF),
        pltpu.VMEM((2, 64, D), BF), pltpu.VMEM((2, 128, F), BF), pltpu.VMEM((2, 4096, TRAIN), BF),
        pltpu.VMEM((32, D), BF), pltpu.VMEM((32, D), BF), pltpu.VMEM((3, 4, 16, 128), BF), pltpu.VMEM((3, 256, 256), BF), pltpu.VMEM((128, 4096), BF),
        pltpu.VMEM((3, 512, 128), BF), pltpu.VMEM((3, 512, 128), BF),
        *three(128), *three(128),
        *three(512), *three(512),
        *three(512), *three(512),
        pltpu.VMEM((512, D), BF), pltpu.VMEM((512, F), BF), pltpu.VMEM((512, F), F32), pltpu.VMEM((512, F), F32),
        pltpu.VMEM((512, F), F32),
        pltpu.VMEM((512, 128), F32), pltpu.VMEM((512, F), BF), pltpu.VMEM((512, F), BF), pltpu.VMEM((512, D), BF),
        pltpu.VMEM((256, 4096), BF), pltpu.VMEM((512, TRAIN), BF),
        *three(512), *three(512),
        *two(512), *two(512),
        *three(128), *two(128),
        pltpu.SemaphoreType.DMA((9,)), pltpu.SemaphoreType.DMA((81,)), pltpu.SemaphoreType.DMA((81,)),
    ]
    done = pl.pallas_call(
        kernel,
        out_shape=[jax.ShapeDtypeStruct((128, w), BF) for w in WIDTH + (256, 256)],
        in_specs=[hbm, hbm, vmem, vmem] + [hbm] * 6,
        out_specs=[hbm] * 5,
        scratch_shapes=scratch,
        compiler_params=pltpu.CompilerParams(
            collective_id=0, has_side_effects=True, vmem_limit_bytes=60 * 1024 * 1024
        ),
        cost_estimate=pl.CostEstimate(flops=9_000_000_000, bytes_accessed=22_000_000, transcendentals=262_144),
    )(
        tokens, out_grad, expert_ids.T, gate_w.T, w_gate, w_up, w_down,
        jnp.swapaxes(proj_out, 1, 2), jnp.swapaxes(proj_in, 1, 2), train_grads,
    )
    return pl.pallas_call(
        close,
        out_shape=(jax.ShapeDtypeStruct((32, D), BF), jax.ShapeDtypeStruct((8, TRAIN), F32)),
        in_specs=[vmem] * 6,
        out_specs=(vmem, vmem),
    )(*done, query_ids)


def solution(mesh):
    rows = P(("group", "expert"), None)
    stack = P(("group", "expert"), None, None)
    return jax.shard_map(
        body,
        mesh=mesh,
        in_specs=(rows,) * 5 + (stack,) * 6,
        out_specs=(rows, rows),
        check_vma=False,
    )
```

```python
import jax
import jax.numpy as jnp
from jax import lax
from jax.experimental import pallas as pl
from jax.experimental.pallas import tpu as pltpu
from jax.sharding import PartitionSpec as P

MESH = pl.DeviceIdType.MESH
BF = jnp.bfloat16
F32 = jnp.float32
COLS = ((0, 640), (640, 1280), (1280, 2048))
SCOLS = ((0, 256), (256, 512), None)
WIDTH = tuple(b - a for a, b in COLS)
STEPS = {
    3: (((0, 128), (0, 128), (0, 256)), ((128, 640), (128, 640), (256, 768))),
    4: (((0, 384), (0, 384), (0, 512)), ((384, 640), (384, 640), (512, 768))),
    5: (((0, 128), (0, 128), (0, 256)), ((128, 384), (128, 384), (256, 512)), ((384, 640), (384, 640), (512, 768))),
    6: (((0, 256), (0, 256)),),
}
LOADS = ((0, 1, 2, 3), (4, 5, 6))
D = 2048
F = 512
TRAIN = 512


def nn(a, b):
    return jnp.dot(a, b, preferred_element_type=F32)


def nt(a, b):
    return lax.dot_general(a, b, (((1,), (1,)), ((), ())), preferred_element_type=F32)


def tn(a, b):
    return lax.dot_general(a, b, (((0,), (0,)), ((), ())), preferred_element_type=F32)


def coords(axis, line, u, v):
    return ((line, u, v), (u, line, v), (u, v, line))[axis]


def device(axis, line, u, v, core):
    y, z, x = coords(axis, line, u, v)
    return (y * 2 + core, z * 4 + x)


def expert_of(axis, line, u, v, core, which):
    group, place = device(axis, line, u, v, core)
    return group * 32 + place * 2 + which


def aligned(start, unit):
    return pl.ds(pl.multiple_of(start * unit, unit), unit)


def kernel(
    tok_h, og_h, ids_ref, gw_ref, wg_h, wu_h, wd_h, po_h, pi_h, tr_h,
    hg0, hg1, hg2, hq0, hq1,
    wg, wu, wd, po, pi, tr,
    tok, og, meta, perm, spread, pick, pickw,
    tx0, tx1, tx2, tg0, tg1, tg2,
    sx0, sx1, sx2, sd0, sd1, sd2,
    rx0, rx1, rx2, rd0, rd1, rd2,
    xc, hid, fa, fb, dh, right, gg, gu, gc, outer, scc,
    gs0, gs1, gs2, gr0, gr1, gr2,
    ss0, ss1, sr0, sr1,
    pg0, pg1, pg2, pq0, pq1,
    load_sem, send_sem, recv_sem,
):
    tx, tg = (tx0, tx1, tx2), (tg0, tg1, tg2)
    sx, sd = (sx0, sx1, sx2), (sd0, sd1, sd2)
    rx, rd = (rx0, rx1, rx2), (rd0, rd1, rd2)
    gs, gr = (gs0, gs1, gs2), (gr0, gr1, gr2)
    ss, sr = (ss0, ss1), (sr0, sr1)
    pg, hg = (pg0, pg1, pg2), (hg0, hg1, hg2)
    pq, hq = (pq0, pq1), (hq0, hq1)
    group, place = lax.axis_index("group"), lax.axis_index("expert")
    y, core = group // 2, group % 2
    z, x = place // 4, place % 4
    line = (y, z, x)
    uv = ((z, x), (y, x), (y, z))
    plane = tuple((u * 4 + v) * 2 + core for u, v in uv)

    loads = [
        pltpu.make_async_copy(src, dst, load_sem.at[n])
        for n, (src, dst) in enumerate(
            (
                (wg_h, wg), (wu_h, wu), (pi_h, pi.at[:, 0:64]), (pi_h, pi.at[:, 64:128]),
                (wd_h, wd), (po_h, po), (tr_h, tr),
            )
        )
    ]

    staged = [pltpu.make_async_copy(src, dst, load_sem.at[7 + n]) for n, (src, dst) in enumerate(((tok_h, tok), (og_h, og)))]
    for copy in staged:
        copy.start()
    barrier = pltpu.get_barrier_semaphore()
    for a in range(3):
        for d in range(1, 4):
            for c in range(2):
                pl.semaphore_signal(
                    barrier, inc=1, device_id=device(a, lax.rem(line[a] + d, 4), uv[a][0], uv[a][1], c), device_id_type=MESH
                )
    pl.semaphore_signal(barrier, inc=1, device_id=(y * 2 + 1 - core, place), device_id_type=MESH)

    own = jnp.concatenate([ids_ref[...].astype(F32), gw_ref[...].astype(F32)], axis=0).astype(BF)
    for a in range(3):
        lane = lax.broadcasted_iota(jnp.int32, (32, 128), 1)
        row = lax.broadcasted_iota(jnp.int32, (32, 128), 0)
        put = jnp.where(lane == row + 32 * line[a], 1.0, 0.0).astype(BF)
        meta[a, pl.ds(line[a], 1)] = nn(own, put).astype(BF)[None]
    pl.semaphore_wait(barrier, 19)

    def spot_of(phase, a, step=0):
        return (phase * 3 + a) * 3 + step

    def line_peers(a):
        for d in range(1, 4):
            there = lax.rem(line[a] + d, 4)
            yield there, device(a, there, uv[a][0], uv[a][1], core)

    def on_line(a, src_of, dst, phase):
        sem = spot_of(phase, a)
        for there, dev in line_peers(a):
            pltpu.make_async_remote_copy(
                src_of(there), dst, send_sem.at[sem], recv_sem.at[sem], device_id=dev, device_id_type=MESH
            ).start()

    def wait_bytes(ref, sem):
        pltpu.make_async_copy(ref, ref, sem).wait()

    for a in range(3):
        on_line(a, lambda there, a=a: meta.at[a, line[a]], meta.at[a, line[a]], 0)
    for n, (phase, src, dst) in enumerate(((1, tok, tx), (2, og, tg))):
        staged[n].wait()
        for a in range(3):
            part = src.at[:, COLS[a][0]:COLS[a][1]]
            spot = dst[a].at[aligned(line[a], 32)]
            on_line(a, lambda there, part=part: part, spot, phase)
            pltpu.make_async_copy(part, spot, recv_sem.at[spot_of(phase, a)]).start()

    r0 = lax.broadcasted_iota(jnp.int32, (128, 128), 0)
    c1 = lax.broadcasted_iota(jnp.int32, (128, 128), 1)
    before = jnp.where((r0 < c1) & ((r0 >> 5) == (c1 >> 5)), 1.0, 0.0).astype(BF)
    r1 = lax.broadcasted_iota(jnp.int32, (1, 8, 128), 1)
    c2 = lax.broadcasted_iota(jnp.int32, (1, 8, 128), 2)
    tile = jnp.where((c2 >> 5) == (r1 >> 1), (r1 & 1) + 1, -1).astype(F32)
    r2 = lax.broadcasted_iota(jnp.int32, (64, 128), 0)

    def choose(a):
        wait_bytes(meta.at[a, 0:3], recv_sem.at[spot_of(0, a)])
        both = (meta[a, 0].astype(F32) + meta[a, 1].astype(F32)) + (meta[a, 2].astype(F32) + meta[a, 3].astype(F32))
        wanted = expert_of(a, line[a], r2 >> 4, (r2 >> 2) & 3, (r2 >> 1) & 1, r2 & 1).astype(F32)
        named = jnp.zeros((64, 128), F32)
        weight = jnp.zeros((64, 128), F32)
        for k in range(8):
            hit = both[k:k + 1, :] == wanted
            named = named + jnp.where(hit, 1.0, 0.0)
            weight = weight + jnp.where(hit, both[8 + k:9 + k, :], 0.0)
        code = named * (nn(named.astype(BF), before) + 1.0)
        taken = jnp.broadcast_to(code[:, None, :], (64, 8, 128)) == tile
        pick[a] = jnp.where(taken, 1.0, 0.0).reshape(512, 128).astype(BF)
        pickw[a] = jnp.where(taken, jnp.broadcast_to(weight[:, None, :], (64, 8, 128)), 0.0).reshape(512, 128).astype(BF)

    def sender(a, src, dst, phase, step):
        sem = spot_of(phase, a, step)
        cols = STEPS[phase][step][a]
        cols = slice(*cols)
        spot = dst.at[aligned(plane[a], 16), cols]

        def send(du, dv, flip):
            u = lax.rem(uv[a][0] + du, 4)
            v = lax.rem(uv[a][1] + dv, 4)
            c = 1 - core if flip else core
            pltpu.make_async_remote_copy(
                src.at[aligned((u * 4 + v) * 2 + c, 16), cols], spot, send_sem.at[sem], recv_sem.at[sem],
                device_id=device(a, line[a], u, v, c), device_id_type=MESH,
            ).start()

        return send, lambda: pltpu.make_async_copy(src.at[aligned(plane[a], 16), cols], spot, recv_sem.at[sem]).start()

    def to_planes(jobs):
        made = [sender(*job) for job in jobs]

        def row(du):
            for dv in (2, 1, 3, 0):
                for flip in range(2):
                    for send, _ in made:
                        send(du, dv, flip)

        def ahead(d, carry):
            row(d)
            return carry
        lax.fori_loop(2, 4, ahead, 0)
        row(1)
        for dv in (2, 1, 3):
            for flip in range(2):
                for send, _ in made:
                    send(0, dv, flip)
        for send, keep in made:
            send(0, 0, 1)
            keep()

    for a in range(3):
        choose(a)
    for phase, chosen, rows, out, into in ((3, pick, tx, sx, rx), (4, pickw, tg, sd, rd)):
        for step, ranges in enumerate(STEPS[phase]):
            for a in range(3):
                if step == 0:
                    wait_bytes(rows[a], recv_sem.at[spot_of(phase - 2, a)])
                cols = slice(*ranges[a])
                for q in range(2):
                    span = slice(q * 256, q * 256 + 256)
                    out[a][span, cols] = nn(chosen[a, span], rows[a][:, cols]).astype(BF)
            to_planes([(a, out[a], into[a], phase, step) for a in range(3)])
        for n in LOADS[phase - 3]:
            loads[n].start()

    for a in range(3):
        for q in range(2):
            n = lax.broadcasted_iota(jnp.int32, (128, 256), 0) + q * 128
            lane = lax.broadcasted_iota(jnp.int32, (128, 256), 1)
            l0, u0, v0 = (
                (n >> 6, (n >> 4) & 3, (n >> 2) & 3), ((n >> 4) & 3, n >> 6, (n >> 2) & 3), ((n >> 2) & 3, n >> 6, (n >> 4) & 3)
            )[a]
            at = ((u0 * 4 + v0) * 2 + ((n >> 1) & 1)) * 8 + l0 * 2 + (n & 1)
            perm[a, q * 128:q * 128 + 128] = jnp.where(lane == at, 1.0, 0.0).astype(BF)
    for q in range(8):
        n = lax.broadcasted_iota(jnp.int32, (128, 512), 0)
        lane = lax.broadcasted_iota(jnp.int32, (128, 512), 1) + q * 512
        spread[:, q * 512:q * 512 + 512] = jnp.where((lane >> 6) == (n & 63), 1.0, 0.0).astype(BF)

    def reorder(got, phase, step):
        for a in range(3):
            start, stop = STEPS[phase][step][a]
            wait_bytes(got[a].at[:, start:stop], recv_sem.at[spot_of(phase, a, step)])
            for k in range(start, stop, 128):
                units = got[a][:, k:k + 128].astype(F32).reshape(32, 2, 8, 128)
                for i in range(2):
                    xc[i * 256:i * 256 + 256, COLS[a][0] + k:COLS[a][0] + k + 128] = nn(
                        perm[a], units[:, i].reshape(256, 128).astype(BF)
                    ).astype(BF)

    def restore(a, rows, out):
        for k in range(0, out.shape[1], 128):
            both = [
                tn(perm[a], rows[i * 256:i * 256 + 256, k:k + 128]).reshape(32, 1, 8, 128) for i in range(2)
            ]
            out[:, k:k + 128] = jnp.concatenate(both, axis=1).reshape(512, 128).astype(BF)

    for step in range(len(STEPS[3])):
        reorder(rx, 3, step)
    for n in range(4):
        loads[n].wait()

    def first(i, carry):
        rows = aligned(i, 256)
        a_gate = nn(xc[rows], wg[i])
        a_up = nn(xc[rows], wu[i])
        sig = jax.nn.sigmoid(a_gate)
        active = a_gate * sig
        fa[rows] = active
        fb[rows] = a_up * sig * (1.0 + a_gate * (1.0 - sig))
        hid[rows] = (active * a_up).astype(BF)
        right[rows] = nt(hid[rows], pi[i])
        return carry
    lax.fori_loop(0, 2, first, 0)

    for n in range(4, 7):
        loads[n].wait()
    for step, ranges in enumerate(STEPS[4]):
        reorder(rd, 4, step)
        for i in range(2):
            rows = slice(i * 256, i * 256 + 256)
            d_hidden = dh[rows] if step else None
            for a in range(3):
                cols = slice(COLS[a][0] + ranges[a][0], COLS[a][0] + ranges[a][1])
                term = nt(xc[rows, cols], wd[i, :, cols])
                d_hidden = term if d_hidden is None else d_hidden + term
            if step < len(STEPS[4]) - 1:
                dh[rows] = d_hidden
            else:
                gu[rows] = (d_hidden * fa[rows]).astype(BF)
                gg[rows] = (d_hidden * fb[rows]).astype(BF)

    for step, ranges in enumerate(STEPS[5]):
        for a in range(3):
            cols = slice(COLS[a][0] + ranges[a][0], COLS[a][0] + ranges[a][1])
            for i in range(2):
                rows = slice(i * 256, i * 256 + 256)
                gc[rows, cols] = (nt(gg[rows], wg[i, cols]) + nt(gu[rows], wu[i, cols])).astype(BF)
            restore(a, gc.at[:, cols], gs[a].at[:, slice(*ranges[a])])
        to_planes([(a, gs[a], gr[a], 5, step) for a in range(3)])

    for i in range(2):
        rows = slice(i * 256, i * 256 + 256)
        left = nt(xc[rows], po[i])
        high = left.astype(BF)
        terms = jnp.concatenate([high, (left - high.astype(F32)).astype(BF)], axis=1)
        twice = right[rows]
        for j in range(8):
            wide = nn(terms, spread[:, 512 * j:512 * j + 512])
            for m in range(4):
                at = 512 * j + 128 * m
                outer[:, at:at + 128] = (wide[:, 128 * m:128 * m + 128] * twice).astype(BF)
        scc[rows] = nn(outer[...], tr[i]).astype(BF)
    for a in range(2):
        restore(a, scc.at[:, SCOLS[a][0]:SCOLS[a][1]], ss[a])
    to_planes([(a, ss[a], sr[a], 6, 0) for a in range(2)])

    def home(parts, got, part, into, phase):
        for step, ranges in enumerate(STEPS[phase]):
            for a in parts:
                cols = slice(*ranges[a])
                wait_bytes(got[a].at[:, cols], recv_sem.at[spot_of(phase, a, step)])
                part[a][:, cols] = tn(pick[a], got[a][:, cols]).astype(BF)
        for a in parts:
            spot = into[a].at[aligned(line[a], 32)]
            on_line(a, lambda there, a=a: part[a].at[aligned(there, 32)], spot, phase + 2)
            pltpu.make_async_copy(
                part[a].at[aligned(line[a], 32)], spot, recv_sem.at[spot_of(phase + 2, a)]
            ).start()

    home(range(3), gr, pg, hg, 5)
    home(range(2), sr, pq, hq, 6)
    for a in range(3):
        wait_bytes(hg[a], recv_sem.at[spot_of(7, a)])
    for a in range(2):
        wait_bytes(hq[a], recv_sem.at[spot_of(8, a)])
    for a in range(3):
        wait_bytes(meta.at[a, 0:3], send_sem.at[spot_of(0, a)])
        wait_bytes(tx[a].at[0:96], send_sem.at[spot_of(1, a)])
        wait_bytes(tg[a].at[0:96], send_sem.at[spot_of(2, a)])
        wait_bytes(pg[a].at[0:96], send_sem.at[spot_of(7, a)])
        for phase, sent in ((3, sx), (4, sd), (5, gs)):
            for step, ranges in enumerate(STEPS[phase]):
                wait_bytes(sent[a].at[0:496, slice(*ranges[a])], send_sem.at[spot_of(phase, a, step)])
    for a in range(2):
        wait_bytes(ss[a].at[0:496], send_sem.at[spot_of(6, a)])
        wait_bytes(pq[a].at[0:96], send_sem.at[spot_of(8, a)])


def close(hg0, hg1, hg2, hq0, hq1, qid_ref, grads_out, scores_out):
    def total(ref):
        return (ref[0:32].astype(F32) + ref[32:64].astype(F32)) + (ref[64:96].astype(F32) + ref[96:128].astype(F32))

    for a, ref in enumerate((hg0, hg1, hg2)):
        grads_out[:, COLS[a][0]:COLS[a][1]] = total(ref).astype(BF)
    query = jnp.where(
        lax.broadcasted_iota(jnp.int32, (8, 32), 0) == jnp.broadcast_to(qid_ref[...], (8, 32)), 1.0, 0.0
    ).astype(F32)
    for a, ref in enumerate((hq0, hq1)):
        scores_out[:, SCOLS[a][0]:SCOLS[a][1]] = jnp.dot(
            query, total(ref), precision=lax.Precision.HIGHEST, preferred_element_type=F32
        )


def body(tokens, out_grad, expert_ids, gate_w, query_ids, w_gate, w_up, w_down, proj_out, proj_in, train_grads):
    vmem = pl.BlockSpec(memory_space=pltpu.VMEM)
    hbm = pl.BlockSpec(memory_space=pl.ANY)

    def three(rows, dtype=BF):
        return [pltpu.VMEM((rows, w), dtype) for w in WIDTH]

    def two(rows):
        return [pltpu.VMEM((rows, s[1] - s[0]), BF) for s in SCOLS if s]

    scratch = [
        pltpu.VMEM((2, D, F), BF), pltpu.VMEM((2, D, F), BF), pltpu.VMEM((2, F, D), BF),
        pltpu.VMEM((2, 64, D), BF), pltpu.VMEM((2, 128, F), BF), pltpu.VMEM((2, 4096, TRAIN), BF),
        pltpu.VMEM((32, D), BF), pltpu.VMEM((32, D), BF), pltpu.VMEM((3, 4, 16, 128), BF), pltpu.VMEM((3, 256, 256), BF), pltpu.VMEM((128, 4096), BF),
        pltpu.VMEM((3, 512, 128), BF), pltpu.VMEM((3, 512, 128), BF),
        *three(128), *three(128),
        *three(512), *three(512),
        *three(512), *three(512),
        pltpu.VMEM((512, D), BF), pltpu.VMEM((512, F), BF), pltpu.VMEM((512, F), F32), pltpu.VMEM((512, F), F32),
        pltpu.VMEM((512, F), F32),
        pltpu.VMEM((512, 128), F32), pltpu.VMEM((512, F), BF), pltpu.VMEM((512, F), BF), pltpu.VMEM((512, D), BF),
        pltpu.VMEM((256, 4096), BF), pltpu.VMEM((512, TRAIN), BF),
        *three(512), *three(512),
        *two(512), *two(512),
        *three(128), *two(128),
        pltpu.SemaphoreType.DMA((9,)), pltpu.SemaphoreType.DMA((81,)), pltpu.SemaphoreType.DMA((81,)),
    ]
    done = pl.pallas_call(
        kernel,
        out_shape=[jax.ShapeDtypeStruct((128, w), BF) for w in WIDTH + (256, 256)],
        in_specs=[hbm, hbm, vmem, vmem] + [hbm] * 6,
        out_specs=[hbm] * 5,
        scratch_shapes=scratch,
        compiler_params=pltpu.CompilerParams(
            collective_id=0, has_side_effects=True, vmem_limit_bytes=60 * 1024 * 1024
        ),
        cost_estimate=pl.CostEstimate(flops=9_000_000_000, bytes_accessed=22_000_000, transcendentals=262_144),
    )(
        tokens, out_grad, expert_ids.T, gate_w.T, w_gate, w_up, w_down,
        jnp.swapaxes(proj_out, 1, 2), jnp.swapaxes(proj_in, 1, 2), train_grads,
    )
    return pl.pallas_call(
        close,
        out_shape=(jax.ShapeDtypeStruct((32, D), BF), jax.ShapeDtypeStruct((8, TRAIN), F32)),
        in_specs=[vmem] * 6,
        out_specs=(vmem, vmem),
    )(*done, query_ids)


def solution(mesh):
    rows = P(("group", "expert"), None)
    stack = P(("group", "expert"), None, None)
    return jax.shard_map(
        body,
        mesh=mesh,
        in_specs=(rows,) * 5 + (stack,) * 6,
        out_specs=(rows, rows),
        check_vma=False,
    )
```
